32 devices in a mesh: gx: 4 (over y, x), gy: 8 (over z, core).
Axes of the slice: x: 2, y: 2, z: 4, core: 2. Of those that a mesh axis runs over, the one named last changes fastest.
Arguments:
- right_side: float32 [16, 1024, 1024], P(None, 'gy', 'gx'), may hold values from -8 to 8
- conduct: float32 [16, 1024, 1024], P(None, 'gy', 'gx'), may hold values from 0.3 to 3
- excavated: int32 [16, 1024, 1024], P(None, 'gy', 'gx'), may hold values 0 or 1
- vectors_x: float32 [1024, 1024], replicated, may hold values from -0.1875 to 0.1875
- mass_x: float32 [1024], P('gy'), may hold values from 0.5 to 2
- values_x: float32 [1024], replicated, may hold values from 0.05 to 5
- vectors_y: float32 [1024, 1024], replicated, may hold values from -0.1875 to 0.1875
- mass_y: float32 [1024], P('gx'), may hold values from 0.5 to 2
- values_y: float32 [1024], replicated, may hold values from 0.05 to 5
- vertical_diag: float32 [16], replicated, may hold values from 3.2 to 4.5
- vertical_coupling: float32 [15], replicated, may hold values from 0.5 to 1.5
Outputs:
- adjoint: float32 [16, 1024, 1024], P(None, 'gy', 'gx')
- residual: float32 [16, 1024, 1024], P(None, 'gy', 'gx')
The draws below stay inside these ranges and needn't reach their ends.
All inputs are finite; a program needn't handle non-finite values. No bound on the sum of `excavated` on one device may be relied on, other than what follows from the above.
Results may differ from the reference program's by a relative error of at most 0.0001.
Values sent between devices are 32-bit elements; how exact they have to be, the bound alone decides.
A program may use at most 128 MiB of HBM per device.

```python
import math
import jax
import jax.numpy as jnp
from jax import lax

NX = 1024
NY = 1024
NZ = 16
ITERS = 2


def place_ends(drawn, stream_key, least, top_value):
    shape = drawn.shape
    spot = [jax.random.randint(jax.random.fold_in(stream_key, axis), (), 0, shape[axis]) for axis in range(len(shape))]
    drawn = drawn.at[tuple(spot)].set(least)
    longest = shape.index(max(shape))
    spot[longest] = (spot[longest] + 1) % shape[longest]
    return drawn.at[tuple(spot)].set(top_value)


def steps_of(stream_key, shape, cuts, least, high):
    factor_of = 1.0
    for dim, shards_of in cuts:
        steps = jax.random.uniform(jax.random.fold_in(jax.random.fold_in(stream_key, 6), dim), (shards_of,), jnp.float32, least / len(cuts), high / len(cuts))
        factor_of = factor_of * jnp.repeat(jnp.exp(steps), shape[dim] // shards_of).reshape((-1,) + (1,) * (len(shape) - 1 - dim))
    return factor_of


def centred(key, shape, deviation, most, cuts=(), kind=jnp.bfloat16):
    values = deviation * jax.random.normal(key, shape, jnp.float32)
    if cuts:
        values = values * steps_of(key, shape, cuts, -0.22, 0.18)
    return jnp.clip(values, -most, most).astype(kind)


def setup_inputs(seed: int = 0) -> dict:
    streams_of = jax.random.split(jax.random.key(seed), 12)
    return {
        "right_side": centred(streams_of[0], (NZ, NX, NY), 1.0, 8.0, ((1, 8), (2, 4)), jnp.float32),
        "conduct": jnp.clip(jnp.exp(math.log(3.0) - 2.3025851 * jax.random.uniform(streams_of[1], (NZ, NX, NY), jnp.float32) ** steps_of(streams_of[1], (NZ, NX, NY), ((1, 8), (2, 4)), -0.2, 0.2)), 0.3, 3.0),
        "excavated": place_ends((jax.random.randint(streams_of[2], (NZ, NX, NY), 0, 2) < 1).astype(jnp.int32), jax.random.fold_in(streams_of[2], 1), 0, 1),
        "vectors_x": centred(streams_of[3], (NX, NX), NX ** -0.5, 0.1875, (), jnp.float32),
        "mass_x": jnp.clip(jnp.exp(math.log(2.0) - 1.3862944 * jax.random.uniform(streams_of[4], (NX,), jnp.float32) ** steps_of(streams_of[4], (NX,), ((0, 8),), -0.2, 0.2)), 0.5, 2.0),
        "values_x": jnp.clip(jnp.exp(jax.random.uniform(streams_of[5], (NX,), jnp.float32, math.log(0.05), math.log(5.0))), 0.05, 5.0),
        "vectors_y": centred(streams_of[6], (NY, NY), NY ** -0.5, 0.1875, (), jnp.float32),
        "mass_y": jnp.clip(jnp.exp(math.log(2.0) - 1.3862944 * jax.random.uniform(streams_of[7], (NY,), jnp.float32) ** steps_of(streams_of[7], (NY,), ((0, 4),), -0.2, 0.2)), 0.5, 2.0),
        "values_y": jnp.clip(jnp.exp(jax.random.uniform(streams_of[8], (NY,), jnp.float32, math.log(0.05), math.log(5.0))), 0.05, 5.0),
        "vertical_diag": jnp.clip(jax.random.uniform(streams_of[9], (NZ,), jnp.float32, 3.2, 4.5), 3.2, 4.5),
        "vertical_coupling": jnp.clip(jax.random.uniform(streams_of[10], (NZ - 1,), jnp.float32, 0.5, 1.5), 0.5, 1.5),
    }


storage_term = 0.2


def harmonic(first, second):
    return 2.0 * first * second / (first + second)


def neighbours(padded):
    return [padded[2:, 1:-1, 1:-1], padded[:-2, 1:-1, 1:-1],
            padded[1:-1, 2:, 1:-1], padded[1:-1, :-2, 1:-1],
            padded[1:-1, 1:-1, 2:], padded[1:-1, 1:-1, :-2]]


def faces_from(padded):
    center = padded[1:-1, 1:-1, 1:-1]
    return [harmonic(center, other) for other in neighbours(padded)]


def stencil(padded, faces):
    center = padded[1:-1, 1:-1, 1:-1]
    result = storage_term * center
    for face, other in zip(faces, neighbours(padded)):
        result = result + face * (center - other)
    return result


def vertical_solve(rhs, diagonal, coupling, shifts):
    count = rhs.shape[0]
    ratios = []
    partial_value = []
    denom = diagonal[0] + shifts
    ratios.append(-coupling[0] / denom)
    partial_value.append(rhs[0] / denom)
    for position in range(1, count):
        denom = diagonal[position] + shifts + coupling[position - 1] * ratios[-1]
        if position < count - 1:
            ratios.append(-coupling[position] / denom)
        partial_value.append((rhs[position] + coupling[position - 1] * partial_value[-1]) / denom)
    solved = [partial_value[count - 1]]
    for position in range(count - 2, -1, -1):
        solved.append(partial_value[position] - ratios[position] * solved[-1])
    return jnp.stack(solved[::-1], axis=0)


def precondition(values, vectors_x, mass_x, values_x, vectors_y, mass_y, values_y, vertical_diag, vertical_coupling):
    highest = lax.Precision.HIGHEST
    scaled = values * mass_x[None, :, None] * mass_y[None, None, :]
    modes = jnp.einsum('zxy,xi->ziy', scaled, vectors_x, precision=highest)
    modes = jnp.einsum('ziy,yj->zij', modes, vectors_y, precision=highest)
    shifts = values_x[:, None] + values_y[None, :]
    solved = vertical_solve(modes, vertical_diag, vertical_coupling, shifts)
    solved = jnp.einsum('zij,yj->ziy', solved, vectors_y, precision=highest)
    return jnp.einsum('ziy,xi->zxy', solved, vectors_x, precision=highest)


def reference(right_side, conduct, excavated, vectors_x, mass_x, values_x, vectors_y, mass_y, values_y, vertical_diag, vertical_coupling):
    active = excavated.astype(jnp.float32)
    faces = faces_from(jnp.pad(conduct, 1))
    adjoint = jnp.zeros_like(right_side)
    residual = right_side
    for iteration in range(ITERS):
        update = precondition(residual, vectors_x, mass_x, values_x, vectors_y, mass_y, values_y, vertical_diag, vertical_coupling)
        adjoint = adjoint + update
        masked = active * update
        image = stencil(jnp.pad(masked, 1), faces) + (1.0 - active) * update
        residual = residual - image
    return adjoint, residual
```

```python
import functools
import jax
import jax.numpy as jnp
from jax import lax
from jax.experimental import pallas as pl
from jax.experimental.pallas import tpu as pltpu
from jax.sharding import PartitionSpec as P

ITERS = 2
LANES = 128
VMEM = pltpu.VMEM

storage_term = 0.2


def padded_2(block, sides, width):
    for axis, dim in sides:
        count = lax.axis_size(axis)
        forward = [(i, i + 1) for i in range(count - 1)]
        backward = [(target, source) for source, target in forward]
        low = lax.ppermute(
            lax.slice_in_dim(block, block.shape[dim] - width, None, axis=dim), axis, forward
        )
        high = lax.ppermute(lax.slice_in_dim(block, 0, width, axis=dim), axis, backward)
        block = jnp.concatenate([low, block, high], axis=dim)
    return block


def harmonic(first, second):
    return 2.0 * first * second / (first + second)


def neighbours(padded):
    return [
        padded[2:, 1:-1, 1:-1],
        padded[:-2, 1:-1, 1:-1],
        padded[1:-1, 2:, 1:-1],
        padded[1:-1, :-2, 1:-1],
        padded[1:-1, 1:-1, 2:],
        padded[1:-1, 1:-1, :-2],
    ]


def faces_from(padded):
    center = padded[1:-1, 1:-1, 1:-1]
    return [harmonic(center, other) for other in neighbours(padded)]


def stencil(padded, faces):
    center = padded[1:-1, 1:-1, 1:-1]
    result = storage_term * center
    for face, other in zip(faces, neighbours(padded)):
        result = result + face * (center - other)
    return result


def pad_vertical(values):
    return jnp.pad(values, ((1, 1), (0, 0), (0, 0)))


def split(value):
    high = value.astype(jnp.bfloat16)
    return high, (value - high.astype(jnp.float32)).astype(jnp.bfloat16)


def dot3(first, second, dims):
    def one(a, b):
        return lax.dot_general(a, b, (dims, ((), ())), preferred_element_type=jnp.float32)

    return one(first[0], second[0]) + (one(first[0], second[1]) + one(first[1], second[0]))


def split_kernel(in_ref, high_ref, low_ref):
    high_ref[...], low_ref[...] = split(in_ref[...])


def split_matrix(matrix):
    rows, columns = matrix.shape
    spec = pl.BlockSpec((rows // 8, columns), lambda i: (i, 0))
    return pl.pallas_call(
        split_kernel,
        grid=(8,),
        out_shape=[jax.ShapeDtypeStruct(matrix.shape, jnp.bfloat16)] * 2,
        in_specs=[spec],
        out_specs=[spec, spec],
    )(matrix)


def forward_y_kernel(in_ref, high_ref, low_ref, out_ref, low_in, high_in):
    sources, count, part = in_ref.shape
    for source in range(sources):
        high, low = split(in_ref[source])
        high_in[:, source * part : (source + 1) * part] = high
        low_in[:, source * part : (source + 1) * part] = low
    modes = high_ref.shape[1]
    width = 256

    @pl.loop(0, modes // width)
    def _(step):
        columns = pl.ds(pl.multiple_of(step * width, width), width)
        out_ref[columns, :] = dot3(
            (high_ref[:, columns], low_ref[:, columns]),
            (high_in[...], low_in[...]),
            ((0,), (1,)),
        )


def forward_y(values, high, low):
    sources, count, part = values.shape
    size = sources * part
    return pl.pallas_call(
        forward_y_kernel,
        out_shape=jax.ShapeDtypeStruct((size, count), jnp.float32),
        in_specs=[pl.BlockSpec(memory_space=VMEM)] * 3,
        out_specs=pl.BlockSpec(memory_space=VMEM),
        scratch_shapes=[VMEM((count, size), jnp.bfloat16)] * 2,
        compiler_params=pltpu.CompilerParams(vmem_limit_bytes=48 << 20),
    )(values, high, low)


def inverse_y_kernel(in_ref, high_ref, low_ref, out_ref, high_in, low_in):
    targets, count, part = out_ref.shape
    moved = jnp.transpose(in_ref[...])
    high_in[...], low_in[...] = split(moved)
    for target in range(targets):
        rows = slice(target * part, (target + 1) * part)
        out_ref[target] = dot3(
            (high_in[...], low_in[...]), (high_ref[rows, :], low_ref[rows, :]), ((1,), (1,))
        )


def inverse_y(values, high, low, targets):
    size, count = values.shape
    return pl.pallas_call(
        inverse_y_kernel,
        out_shape=jax.ShapeDtypeStruct((targets, count, size // targets), jnp.float32),
        in_specs=[pl.BlockSpec(memory_space=VMEM)] * 3,
        out_specs=pl.BlockSpec(memory_space=VMEM),
        scratch_shapes=[VMEM((count, size), jnp.bfloat16)] * 2,
        compiler_params=pltpu.CompilerParams(vmem_limit_bytes=48 << 20),
    )(values, high, low)


def swap_blocks(tiles, part):
    count = len(tiles)
    lane = lax.broadcasted_iota(jnp.int32, tiles[0].shape, 1) // part
    result = []
    for a in range(count):
        made = None
        for b in range(count):
            shift = ((b - a) * part) % LANES
            moved = pltpu.roll(tiles[b], shift, 1) if shift else tiles[b]
            made = moved if made is None else jnp.where(lane == b, moved, made)
        result.append(made)
    return result


def middle_kernel(
    in_ref, high_ref, low_ref, values_x_ref, values_y_ref, diag_ref, coup_ref, out_ref,
    high_in, low_in, work, ratios,
):
    devices, modes, packed = in_ref.shape
    levels = diag_ref.shape[0]
    part = packed // levels
    group = LANES // part
    size = devices * part
    for tile in range(packed // LANES):
        lanes = slice(tile * LANES, (tile + 1) * LANES)

        @pl.loop(0, devices // group)
        def _(g):
            tiles = [in_ref[g * group + b, :, lanes] for b in range(group)]
            columns = pl.ds(pl.multiple_of(g * LANES, LANES), LANES)
            for a, made in enumerate(swap_blocks(tiles, part)):
                rows = slice((tile * group + a) * modes, (tile * group + a + 1) * modes)
                work[rows, columns] = made

    high_in[...], low_in[...] = split(work[...])
    width = 256

    @pl.loop(0, size // width)
    def _(step):
        columns = pl.ds(pl.multiple_of(step * width, width), width)
        work[:, columns] = dot3(
            (high_in[...], low_in[...]), (high_ref[:, columns], low_ref[:, columns]), ((1,), (0,))
        )

    wide = 512

    @pl.loop(0, size // wide)
    def _(step):
        columns = pl.ds(pl.multiple_of(step * wide, wide), wide)
        for start in range(0, modes, 8):
            shifts = values_x_ref[:, columns] + values_y_ref[start : start + 8, :]
            ratio = partial = None
            for z in range(levels):
                rows = slice(z * modes + start, z * modes + start + 8)
                denom = diag_ref[z] + shifts
                rhs = work[rows, columns]
                if z:
                    denom = denom + coup_ref[z - 1] * ratio
                    rhs = rhs + coup_ref[z - 1] * partial
                inverse = 1.0 / denom
                partial = rhs * inverse
                work[rows, columns] = partial
                if z < levels - 1:
                    ratio = -coup_ref[z] * inverse
                    ratios[rows, columns] = ratio
            solved = partial
            for z in range(levels - 1, -1, -1):
                rows = slice(z * modes + start, z * modes + start + 8)
                if z < levels - 1:
                    solved = work[rows, columns] - ratios[rows, columns] * solved
                work[rows, columns] = solved

    high_in[...], low_in[...] = split(work[...])

    @pl.loop(0, size // width)
    def _(step):
        rows = pl.ds(pl.multiple_of(step * width, width), width)
        work[:, rows] = dot3(
            (high_in[...], low_in[...]), (high_ref[rows, :], low_ref[rows, :]), ((1,), (1,))
        )

    for tile in range(packed // LANES):
        lanes = slice(tile * LANES, (tile + 1) * LANES)

        @pl.loop(0, devices // group)
        def _(g):
            columns = pl.ds(pl.multiple_of(g * LANES, LANES), LANES)
            tiles = [
                work[(tile * group + a) * modes : (tile * group + a + 1) * modes, columns]
                for a in range(group)
            ]
            for b, made in enumerate(swap_blocks(tiles, part)):
                out_ref[g * group + b, :, lanes] = made


def middle(values, high, low, values_x, values_y, diag, coup):
    devices, modes, packed = values.shape
    size = high.shape[0]
    count = modes * diag.shape[0]
    vmem = pl.BlockSpec(memory_space=VMEM)
    smem = pl.BlockSpec(memory_space=pltpu.SMEM)
    return pl.pallas_call(
        middle_kernel,
        out_shape=jax.ShapeDtypeStruct(values.shape, jnp.float32),
        in_specs=[vmem] * 5 + [smem] * 2,
        out_specs=vmem,
        scratch_shapes=[VMEM((count, size), jnp.bfloat16)] * 2
        + [VMEM((count, size), jnp.float32)] * 2,
        compiler_params=pltpu.CompilerParams(vmem_limit_bytes=48 << 20),
    )(values, high, low, values_x[None, :], values_y[:, None], diag, coup)


def shards(
    right_side,
    conduct,
    excavated,
    vectors_x,
    mass_x,
    values_x,
    vectors_y,
    mass_y,
    values_y,
    vertical_diag,
    vertical_coupling,
):
    columns, lines = lax.axis_size("gx"), lax.axis_size("gy")
    devices = columns * lines
    levels, rows, part_y = right_side.shape
    part_x = rows // columns
    modes = vectors_y.shape[1] // devices
    both = ("gy", "gx")
    active = excavated.astype(jnp.float32)
    rim_conduct = padded_2(conduct, (("gy", 1), ("gx", 2)), 1)
    faces = faces_from(pad_vertical(rim_conduct))
    high_x, low_x = split_matrix(vectors_x)
    high_y, low_y = split_matrix(vectors_y)
    start = (lax.axis_index("gy") * columns + lax.axis_index("gx")) * modes
    local_values = lax.dynamic_slice_in_dim(values_y, start, modes, 0)
    adjoint = jnp.zeros_like(right_side)
    residual = right_side
    for iteration in range(ITERS):
        scaled = residual * mass_x[None, :, None] * mass_y[None, None, :]
        scaled = scaled.reshape(levels, columns, part_x, part_y).transpose(1, 0, 2, 3)
        scaled = scaled.reshape(columns, levels * part_x, part_y)
        got = lax.all_to_all(scaled, "gx", split_axis=0, concat_axis=0, tiled=True)
        lines_y = forward_y(got, high_y, low_y)
        lines_y = lines_y.reshape(devices, modes, levels * part_x)
        got = lax.all_to_all(lines_y, both, split_axis=0, concat_axis=0, tiled=True)
        solved = middle(
            got, high_x, low_x, values_x, local_values, vertical_diag, vertical_coupling
        )
        got = lax.all_to_all(solved, both, split_axis=0, concat_axis=0, tiled=True)
        got = got.reshape(devices * modes, levels * part_x)
        back = inverse_y(got, high_y, low_y, columns)
        back = lax.all_to_all(back, "gx", split_axis=0, concat_axis=0, tiled=True)
        back = back.reshape(columns, levels, part_x, part_y).transpose(1, 0, 2, 3)
        update = back.reshape(levels, rows, part_y)
        adjoint = adjoint + update
        masked = active * update
        rim_masked = padded_2(masked, (("gy", 1), ("gx", 2)), 1)
        image = stencil(pad_vertical(rim_masked), faces) + (1.0 - active) * update
        residual = residual - image
    return (adjoint, residual)


def solution(mesh):
    in_specs = (
        P(None, "gy", "gx"),
        P(None, "gy", "gx"),
        P(None, "gy", "gx"),
        P(),
        P("gy"),
        P(),
        P(),
        P("gx"),
        P(),
        P(),
        P(),
    )
    out_specs = (P(None, "gy", "gx"), P(None, "gy", "gx"))
    return jax.shard_map(shards, mesh=mesh, in_specs=in_specs, out_specs=out_specs, check_vma=False)
```

```python
import functools
import jax
import jax.numpy as jnp
from jax import lax
from jax.experimental import pallas as pl
from jax.experimental.pallas import tpu as pltpu
from jax.sharding import PartitionSpec as P

ITERS = 2
LANES = 128
VMEM = pltpu.VMEM

storage_term = 0.2


def harmonic(first, second):
    return 2.0 * first * second / (first + second)


def apply_kernel(
    first, scale, back_ref, conduct_ref, active_ref, residual_ref, *refs
):
    refs = list(refs)
    adjoint_ref = None if first else refs.pop(0)
    mass_x_ref, mass_y_ref = (refs.pop(0), refs.pop(0)) if scale else (None, None)
    new_adjoint_ref, new_residual_ref = refs.pop(0), refs.pop(0)
    scaled_ref = refs.pop(0) if scale else None
    masked, held, out_x, in_x, out_y, in_y, send_sem, recv_sem = refs
    levels, rows, part_y = conduct_ref.shape
    columns, part_x = back_ref.shape[0], back_ref.shape[2]
    ix, iy = lax.axis_index("gx"), lax.axis_index("gy")
    nx, ny = lax.axis_size("gx"), lax.axis_size("gy")
    sides = [
        (lax.rem(iy + 1, ny), ix, iy),
        (lax.rem(iy + ny - 1, ny), ix, iy),
        (iy, lax.rem(ix + 1, nx), ix),
        (iy, lax.rem(ix + nx - 1, nx), ix),
    ]
    barrier = pltpu.get_barrier_semaphore()
    for line, column, _ in sides:
        pl.semaphore_signal(
            barrier, inc=1, device_id=(column, line), device_id_type=pl.DeviceIdType.MESH
        )

    out_y[...] = jnp.zeros_like(out_y)
    for plane in (0, levels + 1):
        masked[plane] = jnp.zeros((rows, part_y), jnp.float32)
        held[plane] = jnp.zeros((rows, part_y), jnp.float32)

    @pl.loop(0, levels)
    def _(z):
        update = jnp.concatenate([back_ref[s, z] for s in range(columns)], axis=0)
        value = active_ref[z].astype(jnp.float32) * update
        conduct = conduct_ref[z]
        masked[z + 1] = value
        held[z + 1] = conduct
        for field, plane in enumerate((value, conduct)):
            at = field * levels + z
            out_x[0, pl.ds(at, 1), :] = plane[rows - 1 :, :]
            out_x[1, pl.ds(at, 1), :] = plane[:1, :]
            out_y[0, pl.ds(at, 1), :rows] = jnp.transpose(plane[:, part_y - LANES :])[LANES - 1 :, :]
            out_y[1, pl.ds(at, 1), :rows] = jnp.transpose(plane[:, :LANES])[:1, :]

    pl.semaphore_wait(barrier, 4)
    copies = []
    for k, (line, column, _) in enumerate(sides):
        source, target = (out_x, in_x) if k < 2 else (out_y, in_y)
        copies.append(
            pltpu.make_async_remote_copy(
                src_ref=source.at[k % 2],
                dst_ref=target.at[k % 2],
                send_sem=send_sem.at[k],
                recv_sem=recv_sem.at[k],
                device_id=(column, line),
                device_id_type=pl.DeviceIdType.MESH,
            )
        )
        copies[-1].start()
    for copy in copies:
        copy.wait()

    inside = [
        jnp.where(iy > 0, 1.0, 0.0),
        jnp.where(iy < ny - 1, 1.0, 0.0),
        jnp.where(ix > 0, 1.0, 0.0),
        jnp.where(ix < nx - 1, 1.0, 0.0),
    ]
    row = lax.broadcasted_iota(jnp.int32, (rows, part_y), 0)
    lane = lax.broadcasted_iota(jnp.int32, (rows, part_y), 1)

    def upright(values):
        tall = jnp.transpose(jnp.broadcast_to(values, (LANES, LANES)))[:rows]
        return jnp.concatenate([tall] * (part_y // LANES), axis=1)

    @pl.loop(0, levels)
    def _(z):
        center, conduct = masked[z + 1], held[z + 1]
        result = storage_term * center

        def add(result, other, other_conduct):
            return result + harmonic(conduct, other_conduct) * (center - other)

        result = add(result, masked[z + 2], held[z + 2])
        result = add(result, masked[z], held[z])
        at, at_conduct = pl.ds(z, 1), pl.ds(levels + z, 1)
        result = add(
            result,
            jnp.where(row == rows - 1, in_x[1, at, :], pltpu.roll(center, rows - 1, 0)),
            jnp.where(
                row == rows - 1, in_x[1, at_conduct, :] * inside[1], pltpu.roll(conduct, rows - 1, 0)
            ),
        )
        result = add(
            result,
            jnp.where(row == 0, in_x[0, at, :], pltpu.roll(center, 1, 0)),
            jnp.where(row == 0, in_x[0, at_conduct, :] * inside[0], pltpu.roll(conduct, 1, 0)),
        )
        result = add(
            result,
            jnp.where(lane == part_y - 1, upright(in_y[1, at, :]), pltpu.roll(center, part_y - 1, 1)),
            jnp.where(
                lane == part_y - 1,
                upright(in_y[1, at_conduct, :]) * inside[3],
                pltpu.roll(conduct, part_y - 1, 1),
            ),
        )
        result = add(
            result,
            jnp.where(lane == 0, upright(in_y[0, at, :]), pltpu.roll(center, 1, 1)),
            jnp.where(
                lane == 0, upright(in_y[0, at_conduct, :]) * inside[2], pltpu.roll(conduct, 1, 1)
            ),
        )
        update = jnp.concatenate([back_ref[s, z] for s in range(columns)], axis=0)
        active = active_ref[z].astype(jnp.float32)
        residual = residual_ref[z] - (result + (1.0 - active) * update)
        new_residual_ref[z] = residual
        new_adjoint_ref[z] = update if first else adjoint_ref[z] + update
        if scale:
            scaled = residual * mass_x_ref[...] * mass_y_ref[...]
            for s in range(columns):
                scaled_ref[s, z] = scaled[s * part_x : (s + 1) * part_x, :]


def apply_update(iteration, back, conduct, excavated, residual, adjoint, mass_x, mass_y):
    first, scale = iteration == 0, iteration < ITERS - 1
    levels, rows, part_y = conduct.shape
    operands = [back, conduct, excavated, residual]
    if not first:
        operands.append(adjoint)
    if scale:
        operands += [mass_x[:, None], mass_y[None, :]]
    field = jax.ShapeDtypeStruct(conduct.shape, jnp.float32)
    outputs = [field, field]
    if scale:
        outputs.append(jax.ShapeDtypeStruct(back.shape, jnp.float32))
    vmem = pl.BlockSpec(memory_space=VMEM)
    return pl.pallas_call(
        functools.partial(apply_kernel, first, scale),
        out_shape=outputs,
        in_specs=[vmem] * len(operands),
        out_specs=[vmem] * len(outputs),
        scratch_shapes=[VMEM((levels + 2, rows, part_y), jnp.float32)] * 2
        + [VMEM((2, 2 * levels, part_y), jnp.float32)] * 2
        + [VMEM((2, 2 * levels, LANES), jnp.float32)] * 2
        + [pltpu.SemaphoreType.DMA((4,))] * 2,
        compiler_params=pltpu.CompilerParams(
            collective_id=iteration, has_side_effects=True, vmem_limit_bytes=48 << 20
        ),
    )(*operands)


def split(value):
    high = value.astype(jnp.bfloat16)
    return high, (value - high.astype(jnp.float32)).astype(jnp.bfloat16)


def dot3(first, second, dims):
    def one(a, b):
        return lax.dot_general(a, b, (dims, ((), ())), preferred_element_type=jnp.float32)

    return one(first[0], second[0]) + (one(first[0], second[1]) + one(first[1], second[0]))


def split_kernel(in_ref, high_ref, low_ref):
    high_ref[...], low_ref[...] = split(in_ref[...])


def split_matrix(matrix):
    rows, columns = matrix.shape
    spec = pl.BlockSpec((rows // 8, columns), lambda i: (i, 0))
    return pl.pallas_call(
        split_kernel,
        grid=(8,),
        out_shape=[jax.ShapeDtypeStruct(matrix.shape, jnp.bfloat16)] * 2,
        in_specs=[spec],
        out_specs=[spec, spec],
    )(matrix)


def forward_y_kernel(in_ref, high_ref, low_ref, out_ref, low_in, high_in):
    sources, count, part = in_ref.shape
    for source in range(sources):
        high, low = split(in_ref[source])
        high_in[:, source * part : (source + 1) * part] = high
        low_in[:, source * part : (source + 1) * part] = low
    modes = high_ref.shape[1]
    width = 256

    @pl.loop(0, modes // width)
    def _(step):
        columns = pl.ds(pl.multiple_of(step * width, width), width)
        out_ref[columns, :] = dot3(
            (high_ref[:, columns], low_ref[:, columns]),
            (high_in[...], low_in[...]),
            ((0,), (1,)),
        )


def forward_y(values, high, low):
    sources, count, part = values.shape
    size = sources * part
    return pl.pallas_call(
        forward_y_kernel,
        out_shape=jax.ShapeDtypeStruct((size, count), jnp.float32),
        in_specs=[pl.BlockSpec(memory_space=VMEM)] * 3,
        out_specs=pl.BlockSpec(memory_space=VMEM),
        scratch_shapes=[VMEM((count, size), jnp.bfloat16)] * 2,
        compiler_params=pltpu.CompilerParams(vmem_limit_bytes=48 << 20),
    )(values, high, low)


def inverse_y_kernel(in_ref, high_ref, low_ref, out_ref, high_in, low_in):
    targets, count, part = out_ref.shape
    moved = jnp.transpose(in_ref[...])
    high_in[...], low_in[...] = split(moved)
    for target in range(targets):
        rows = slice(target * part, (target + 1) * part)
        out_ref[target] = dot3(
            (high_in[...], low_in[...]), (high_ref[rows, :], low_ref[rows, :]), ((1,), (1,))
        )


def inverse_y(values, high, low, targets):
    size, count = values.shape
    return pl.pallas_call(
        inverse_y_kernel,
        out_shape=jax.ShapeDtypeStruct((targets, count, size // targets), jnp.float32),
        in_specs=[pl.BlockSpec(memory_space=VMEM)] * 3,
        out_specs=pl.BlockSpec(memory_space=VMEM),
        scratch_shapes=[VMEM((count, size), jnp.bfloat16)] * 2,
        compiler_params=pltpu.CompilerParams(vmem_limit_bytes=48 << 20),
    )(values, high, low)


def swap_blocks(tiles, part):
    count = len(tiles)
    lane = lax.broadcasted_iota(jnp.int32, tiles[0].shape, 1) // part
    result = []
    for a in range(count):
        made = None
        for b in range(count):
            shift = ((b - a) * part) % LANES
            moved = pltpu.roll(tiles[b], shift, 1) if shift else tiles[b]
            made = moved if made is None else jnp.where(lane == b, moved, made)
        result.append(made)
    return result


def middle_kernel(
    in_ref, high_ref, low_ref, values_x_ref, values_y_ref, diag_ref, coup_ref, out_ref,
    high_in, low_in, work, ratios,
):
    devices, modes, packed = in_ref.shape
    levels = diag_ref.shape[0]
    part = packed // levels
    group = LANES // part
    size = devices * part
    for tile in range(packed // LANES):
        lanes = slice(tile * LANES, (tile + 1) * LANES)

        @pl.loop(0, devices // group)
        def _(g):
            tiles = [in_ref[g * group + b, :, lanes] for b in range(group)]
            columns = pl.ds(pl.multiple_of(g * LANES, LANES), LANES)
            for a, made in enumerate(swap_blocks(tiles, part)):
                rows = slice((tile * group + a) * modes, (tile * group + a + 1) * modes)
                work[rows, columns] = made

    high_in[...], low_in[...] = split(work[...])
    width = 256

    @pl.loop(0, size // width)
    def _(step):
        columns = pl.ds(pl.multiple_of(step * width, width), width)
        work[:, columns] = dot3(
            (high_in[...], low_in[...]), (high_ref[:, columns], low_ref[:, columns]), ((1,), (0,))
        )

    wide = 512

    @pl.loop(0, size // wide)
    def _(step):
        columns = pl.ds(pl.multiple_of(step * wide, wide), wide)
        for start in range(0, modes, 8):
            shifts = values_x_ref[:, columns] + values_y_ref[start : start + 8, :]
            ratio = partial = None
            for z in range(levels):
                rows = slice(z * modes + start, z * modes + start + 8)
                denom = diag_ref[z] + shifts
                rhs = work[rows, columns]
                if z:
                    denom = denom + coup_ref[z - 1] * ratio
                    rhs = rhs + coup_ref[z - 1] * partial
                inverse = 1.0 / denom
                partial = rhs * inverse
                work[rows, columns] = partial
                if z < levels - 1:
                    ratio = -coup_ref[z] * inverse
                    ratios[rows, columns] = ratio
            solved = partial
            for z in range(levels - 1, -1, -1):
                rows = slice(z * modes + start, z * modes + start + 8)
                if z < levels - 1:
                    solved = work[rows, columns] - ratios[rows, columns] * solved
                work[rows, columns] = solved

    high_in[...], low_in[...] = split(work[...])

    @pl.loop(0, size // width)
    def _(step):
        rows = pl.ds(pl.multiple_of(step * width, width), width)
        work[:, rows] = dot3(
            (high_in[...], low_in[...]), (high_ref[rows, :], low_ref[rows, :]), ((1,), (1,))
        )

    for tile in range(packed // LANES):
        lanes = slice(tile * LANES, (tile + 1) * LANES)

        @pl.loop(0, devices // group)
        def _(g):
            columns = pl.ds(pl.multiple_of(g * LANES, LANES), LANES)
            tiles = [
                work[(tile * group + a) * modes : (tile * group + a + 1) * modes, columns]
                for a in range(group)
            ]
            for b, made in enumerate(swap_blocks(tiles, part)):
                out_ref[g * group + b, :, lanes] = made


def middle(values, high, low, values_x, values_y, diag, coup):
    devices, modes, packed = values.shape
    size = high.shape[0]
    count = modes * diag.shape[0]
    vmem = pl.BlockSpec(memory_space=VMEM)
    smem = pl.BlockSpec(memory_space=pltpu.SMEM)
    return pl.pallas_call(
        middle_kernel,
        out_shape=jax.ShapeDtypeStruct(values.shape, jnp.float32),
        in_specs=[vmem] * 5 + [smem] * 2,
        out_specs=vmem,
        scratch_shapes=[VMEM((count, size), jnp.bfloat16)] * 2
        + [VMEM((count, size), jnp.float32)] * 2,
        compiler_params=pltpu.CompilerParams(vmem_limit_bytes=48 << 20),
    )(values, high, low, values_x[None, :], values_y[:, None], diag, coup)


def shards(
    right_side,
    conduct,
    excavated,
    vectors_x,
    mass_x,
    values_x,
    vectors_y,
    mass_y,
    values_y,
    vertical_diag,
    vertical_coupling,
):
    columns, lines = lax.axis_size("gx"), lax.axis_size("gy")
    devices = columns * lines
    levels, rows, part_y = right_side.shape
    part_x = rows // columns
    modes = vectors_y.shape[1] // devices
    both = ("gy", "gx")
    high_x, low_x = split_matrix(vectors_x)
    high_y, low_y = split_matrix(vectors_y)
    start = (lax.axis_index("gy") * columns + lax.axis_index("gx")) * modes
    local_values = lax.dynamic_slice_in_dim(values_y, start, modes, 0)
    adjoint = None
    residual = right_side
    scaled = residual * mass_x[None, :, None] * mass_y[None, None, :]
    scaled = scaled.reshape(levels, columns, part_x, part_y).transpose(1, 0, 2, 3)
    for iteration in range(ITERS):
        scaled = scaled.reshape(columns, levels * part_x, part_y)
        got = lax.all_to_all(scaled, "gx", split_axis=0, concat_axis=0, tiled=True)
        lines_y = forward_y(got, high_y, low_y)
        lines_y = lines_y.reshape(devices, modes, levels * part_x)
        got = lax.all_to_all(lines_y, both, split_axis=0, concat_axis=0, tiled=True)
        solved = middle(
            got, high_x, low_x, values_x, local_values, vertical_diag, vertical_coupling
        )
        got = lax.all_to_all(solved, both, split_axis=0, concat_axis=0, tiled=True)
        got = got.reshape(devices * modes, levels * part_x)
        back = inverse_y(got, high_y, low_y, columns)
        back = lax.all_to_all(back, "gx", split_axis=0, concat_axis=0, tiled=True)
        back = back.reshape(columns, levels, part_x, part_y)
        adjoint, residual, *rest = apply_update(
            iteration, back, conduct, excavated, residual, adjoint, mass_x, mass_y
        )
        scaled = rest[0] if rest else None
    return (adjoint, residual)


def solution(mesh):
    in_specs = (
        P(None, "gy", "gx"),
        P(None, "gy", "gx"),
        P(None, "gy", "gx"),
        P(),
        P("gy"),
        P(),
        P(),
        P("gx"),
        P(),
        P(),
        P(),
    )
    out_specs = (P(None, "gy", "gx"), P(None, "gy", "gx"))
    return jax.shard_map(shards, mesh=mesh, in_specs=in_specs, out_specs=out_specs, check_vma=False)
```

```python
import functools
import jax
import jax.numpy as jnp
from jax import lax
from jax.experimental import pallas as pl
from jax.experimental.pallas import tpu as pltpu
from jax.sharding import PartitionSpec as P

ITERS = 2
LANES = 128
VMEM = pltpu.VMEM

storage_term = 0.2


def harmonic(first, second):
    return 2.0 * first * second / (first + second)


def apply_kernel(
    first, scale, back_ref, conduct_ref, active_ref, residual_ref, *refs
):
    refs = list(refs)
    adjoint_ref = None if first else refs.pop(0)
    mass_x_ref, mass_y_ref = (refs.pop(0), refs.pop(0)) if scale else (None, None)
    new_adjoint_ref, new_residual_ref = refs.pop(0), refs.pop(0)
    scaled_ref = refs.pop(0) if scale else None
    masked, held, out_x, in_x, out_y, in_y, send_sem, recv_sem = refs
    levels, rows, part_y = conduct_ref.shape
    columns, part_x = back_ref.shape[0], back_ref.shape[2]
    ix, iy = lax.axis_index("gx"), lax.axis_index("gy")
    nx, ny = lax.axis_size("gx"), lax.axis_size("gy")
    sides = [
        (lax.rem(iy + 1, ny), ix, iy),
        (lax.rem(iy + ny - 1, ny), ix, iy),
        (iy, lax.rem(ix + 1, nx), ix),
        (iy, lax.rem(ix + nx - 1, nx), ix),
    ]
    barrier = pltpu.get_barrier_semaphore()
    for line, column, _ in sides:
        pl.semaphore_signal(
            barrier, inc=1, device_id=(column, line), device_id_type=pl.DeviceIdType.MESH
        )

    out_y[...] = jnp.zeros_like(out_y)
    for plane in (0, levels + 1):
        masked[plane] = jnp.zeros((rows, part_y), jnp.float32)
        held[plane] = jnp.zeros((rows, part_y), jnp.float32)

    @pl.loop(0, levels)
    def _(z):
        update = jnp.concatenate([back_ref[s, z] for s in range(columns)], axis=0)
        value = active_ref[z].astype(jnp.float32) * update
        conduct = conduct_ref[z]
        masked[z + 1] = value
        held[z + 1] = conduct
        for field, plane in enumerate((value, conduct)):
            at = field * levels + z
            out_x[0, pl.ds(at, 1), :] = plane[rows - 1 :, :]
            out_x[1, pl.ds(at, 1), :] = plane[:1, :]
            out_y[0, pl.ds(at, 1), :rows] = jnp.transpose(plane[:, part_y - LANES :])[LANES - 1 :, :]
            out_y[1, pl.ds(at, 1), :rows] = jnp.transpose(plane[:, :LANES])[:1, :]

    pl.semaphore_wait(barrier, 4)
    copies = []
    for k, (line, column, _) in enumerate(sides):
        source, target = (out_x, in_x) if k < 2 else (out_y, in_y)
        copies.append(
            pltpu.make_async_remote_copy(
                src_ref=source.at[k % 2],
                dst_ref=target.at[k % 2],
                send_sem=send_sem.at[k],
                recv_sem=recv_sem.at[k],
                device_id=(column, line),
                device_id_type=pl.DeviceIdType.MESH,
            )
        )
        copies[-1].start()
    for copy in copies:
        copy.wait()

    inside = [
        jnp.where(iy > 0, 1.0, 0.0),
        jnp.where(iy < ny - 1, 1.0, 0.0),
        jnp.where(ix > 0, 1.0, 0.0),
        jnp.where(ix < nx - 1, 1.0, 0.0),
    ]
    row = lax.broadcasted_iota(jnp.int32, (rows, part_y), 0)
    lane = lax.broadcasted_iota(jnp.int32, (rows, part_y), 1)

    def upright(values):
        tall = jnp.transpose(jnp.broadcast_to(values, (LANES, LANES)))[:rows]
        return jnp.concatenate([tall] * (part_y // LANES), axis=1)

    @pl.loop(0, levels)
    def _(z):
        center, conduct = masked[z + 1], held[z + 1]
        result = storage_term * center

        def add(result, other, other_conduct):
            return result + harmonic(conduct, other_conduct) * (center - other)

        result = add(result, masked[z + 2], held[z + 2])
        result = add(result, masked[z], held[z])
        at, at_conduct = pl.ds(z, 1), pl.ds(levels + z, 1)
        result = add(
            result,
            jnp.where(row == rows - 1, in_x[1, at, :], pltpu.roll(center, rows - 1, 0)),
            jnp.where(
                row == rows - 1, in_x[1, at_conduct, :] * inside[1], pltpu.roll(conduct, rows - 1, 0)
            ),
        )
        result = add(
            result,
            jnp.where(row == 0, in_x[0, at, :], pltpu.roll(center, 1, 0)),
            jnp.where(row == 0, in_x[0, at_conduct, :] * inside[0], pltpu.roll(conduct, 1, 0)),
        )
        result = add(
            result,
            jnp.where(lane == part_y - 1, upright(in_y[1, at, :]), pltpu.roll(center, part_y - 1, 1)),
            jnp.where(
                lane == part_y - 1,
                upright(in_y[1, at_conduct, :]) * inside[3],
                pltpu.roll(conduct, part_y - 1, 1),
            ),
        )
        result = add(
            result,
            jnp.where(lane == 0, upright(in_y[0, at, :]), pltpu.roll(center, 1, 1)),
            jnp.where(
                lane == 0, upright(in_y[0, at_conduct, :]) * inside[2], pltpu.roll(conduct, 1, 1)
            ),
        )
        update = jnp.concatenate([back_ref[s, z] for s in range(columns)], axis=0)
        active = active_ref[z].astype(jnp.float32)
        residual = residual_ref[z] - (result + (1.0 - active) * update)
        new_residual_ref[z] = residual
        new_adjoint_ref[z] = update if first else adjoint_ref[z] + update
        if scale:
            scaled = residual * mass_x_ref[...] * mass_y_ref[...]
            for s in range(columns):
                scaled_ref[s, z] = scaled[s * part_x : (s + 1) * part_x, :]


def apply_update(iteration, back, conduct, excavated, residual, adjoint, mass_x, mass_y):
    first, scale = iteration == 0, iteration < ITERS - 1
    levels, rows, part_y = conduct.shape
    operands = [back, conduct, excavated, residual]
    if not first:
        operands.append(adjoint)
    if scale:
        operands += [mass_x[:, None], mass_y[None, :]]
    field = jax.ShapeDtypeStruct(conduct.shape, jnp.float32)
    outputs = [field, field]
    if scale:
        outputs.append(jax.ShapeDtypeStruct(back.shape, jnp.float32))
    vmem = pl.BlockSpec(memory_space=VMEM)
    return pl.pallas_call(
        functools.partial(apply_kernel, first, scale),
        out_shape=outputs,
        in_specs=[vmem] * len(operands),
        out_specs=[vmem] * len(outputs),
        scratch_shapes=[VMEM((levels + 2, rows, part_y), jnp.float32)] * 2
        + [VMEM((2, 2 * levels, part_y), jnp.float32)] * 2
        + [VMEM((2, 2 * levels, LANES), jnp.float32)] * 2
        + [pltpu.SemaphoreType.DMA((4,))] * 2,
        compiler_params=pltpu.CompilerParams(
            collective_id=iteration, has_side_effects=True, vmem_limit_bytes=48 << 20
        ),
    )(*operands)


def split(value):
    high = value.astype(jnp.bfloat16)
    return high, (value - high.astype(jnp.float32)).astype(jnp.bfloat16)


def dot3(first, second, dims):
    def one(a, b):
        return lax.dot_general(a, b, (dims, ((), ())), preferred_element_type=jnp.float32)

    return one(first[0], second[0]) + (one(first[0], second[1]) + one(first[1], second[0]))


def split_kernel(in_ref, high_ref, low_ref):
    high_ref[...], low_ref[...] = split(in_ref[...])


def split_matrix(matrix):
    rows, columns = matrix.shape
    spec = pl.BlockSpec((rows // 8, columns), lambda i: (i, 0))
    return pl.pallas_call(
        split_kernel,
        grid=(8,),
        out_shape=[jax.ShapeDtypeStruct(matrix.shape, jnp.bfloat16)] * 2,
        in_specs=[spec],
        out_specs=[spec, spec],
    )(matrix)


MESH = pl.DeviceIdType.MESH


def place():
    columns, lines = lax.axis_size("gx"), lax.axis_size("gy")
    ix, iy = lax.axis_index("gx"), lax.axis_index("gy")
    return columns, columns * lines, ix, iy, iy * columns + ix


def greet_all():
    columns, devices, _, _, me = place()
    barrier = pltpu.get_barrier_semaphore()

    @pl.loop(1, devices)
    def _(k):
        to = lax.rem(me + k, devices)
        pl.semaphore_signal(
            barrier, inc=1, device_id=(lax.rem(to, columns), to // columns), device_id_type=MESH
        )

    pl.semaphore_wait(barrier, devices - 1)


def send_to_all(source_ref, target_ref, lanes, send_sem, recv_sem):
    columns, devices, _, _, me = place()

    @pl.loop(1, devices)
    def _(k):
        to = lax.rem(me + k, devices)
        pltpu.make_async_remote_copy(
            src_ref=source_ref.at[to, :, lanes],
            dst_ref=target_ref.at[me, :, lanes],
            send_sem=send_sem,
            recv_sem=recv_sem,
            device_id=(lax.rem(to, columns), to // columns),
            device_id_type=MESH,
        ).start()


def wait_for_all(ref, lanes, sem):
    part = ref.at[pl.ds(0, ref.shape[0] - 1), :, lanes]
    pltpu.make_async_copy(part, part, sem).wait()


def row_copies(source_ref, target_ref, rows, send_sem, recv_sem):
    columns, _, ix, iy, _ = place()
    copies = []
    for k in range(1, columns):
        to = lax.rem(ix + k, columns)
        copies.append(
            pltpu.make_async_remote_copy(
                src_ref=source_ref.at[to, rows],
                dst_ref=target_ref.at[ix, rows],
                send_sem=send_sem.at[k - 1],
                recv_sem=recv_sem.at[k - 1],
                device_id=(to, iy),
                device_id_type=MESH,
            )
        )
    return copies


def forward_kernel(
    in_ref, high_ref, low_ref, out_ref, got, lines, high_in, low_in, send_x, recv_x, send_all, recv_all
):
    sources, count, part = in_ref.shape
    devices, modes, _ = out_ref.shape
    _, _, ix, _, me = place()
    chunks = count // LANES
    width = 256
    greet_all()
    copies = []
    for chunk in range(chunks):
        rows = slice(chunk * LANES, (chunk + 1) * LANES)
        copies.append(row_copies(in_ref, got, rows, send_x.at[chunk], recv_x.at[chunk]))
        for copy in copies[-1]:
            copy.start()
    got[ix] = in_ref[ix]
    for chunk in range(chunks):
        rows = slice(chunk * LANES, (chunk + 1) * LANES)
        for copy in copies[chunk]:
            copy.wait_recv()
        for source in range(sources):
            along = slice(source * part, (source + 1) * part)
            high_in[:, along], low_in[:, along] = split(got[source, rows, :])

        @pl.loop(0, devices * modes // width)
        def _(step):
            columns = pl.ds(pl.multiple_of(step * width, width), width)
            made = dot3(
                (high_ref[:, columns], low_ref[:, columns]),
                (high_in[...], low_in[...]),
                ((0,), (1,)),
            )
            blocks = width // modes
            lines[pl.ds(step * blocks, blocks), :, rows] = made.reshape(blocks, modes, LANES)

        send_to_all(lines, out_ref, rows, send_all.at[chunk], recv_all.at[chunk])
        out_ref[me, :, rows] = lines[me, :, rows]
    for chunk in range(chunks):
        rows = slice(chunk * LANES, (chunk + 1) * LANES)
        for copy in copies[chunk]:
            copy.wait_send()
        wait_for_all(lines, rows, send_all.at[chunk])
        wait_for_all(out_ref, rows, recv_all.at[chunk])


def inverse_kernel(
    in_ref, high_ref, low_ref, out_ref, got, made, high_in, low_in, send_x, recv_x, send_all, recv_all
):
    targets, count, part = out_ref.shape
    devices, modes, _ = in_ref.shape
    _, _, ix, _, me = place()
    chunks = count // LANES
    greet_all()
    for chunk in range(chunks):
        rows = slice(chunk * LANES, (chunk + 1) * LANES)
        send_to_all(in_ref, got, rows, send_all.at[chunk], recv_all.at[chunk])
    got[me] = in_ref[me]
    copies = []
    for chunk in range(chunks):
        rows = slice(chunk * LANES, (chunk + 1) * LANES)
        wait_for_all(got, rows, recv_all.at[chunk])
        moved = jnp.transpose(got[:, :, rows].reshape(devices * modes, LANES))
        high_in[...], low_in[...] = split(moved)

        @pl.loop(0, targets)
        def _(target):
            along = pl.ds(pl.multiple_of(target * part, part), part)
            made[target, rows, :] = dot3(
                (high_in[...], low_in[...]), (high_ref[along, :], low_ref[along, :]), ((1,), (1,))
            )

        copies.append(row_copies(made, out_ref, rows, send_x.at[chunk], recv_x.at[chunk]))
        for copy in copies[-1]:
            copy.start()
        out_ref[ix, rows, :] = made[ix, rows, :]
    for chunk in range(chunks):
        rows = slice(chunk * LANES, (chunk + 1) * LANES)
        for copy in copies[chunk]:
            copy.wait()
        wait_for_all(in_ref, rows, send_all.at[chunk])


def y_transform(kernel, collective_id, values, high, low, rows_shape, lines_shape, forward):
    count, size = rows_shape[1], high.shape[0]
    chunks = count // LANES
    rows_vmem, lines_vmem = VMEM(rows_shape, jnp.float32), VMEM(lines_shape, jnp.float32)
    row_sems = pltpu.SemaphoreType.DMA((chunks, rows_shape[0] - 1))
    return pl.pallas_call(
        kernel,
        out_shape=jax.ShapeDtypeStruct(lines_shape if forward else rows_shape, jnp.float32),
        in_specs=[pl.BlockSpec(memory_space=VMEM)] * 3,
        out_specs=pl.BlockSpec(memory_space=VMEM),
        scratch_shapes=([rows_vmem, lines_vmem] if forward else [lines_vmem, rows_vmem])
        + [VMEM((LANES, size), jnp.bfloat16)] * 2
        + [row_sems] * 2
        + [pltpu.SemaphoreType.DMA((chunks,))] * 2,
        compiler_params=pltpu.CompilerParams(
            collective_id=collective_id, has_side_effects=True, vmem_limit_bytes=48 << 20
        ),
    )(values, high, low)


def swap_blocks(tiles, part):
    count = len(tiles)
    lane = lax.broadcasted_iota(jnp.int32, tiles[0].shape, 1) // part
    result = []
    for a in range(count):
        made = None
        for b in range(count):
            shift = ((b - a) * part) % LANES
            moved = pltpu.roll(tiles[b], shift, 1) if shift else tiles[b]
            made = moved if made is None else jnp.where(lane == b, moved, made)
        result.append(made)
    return result


def middle_kernel(
    in_ref, high_ref, low_ref, values_x_ref, values_y_ref, diag_ref, coup_ref, out_ref,
    high_in, low_in, work, ratios,
):
    devices, modes, packed = in_ref.shape
    levels = diag_ref.shape[0]
    part = packed // levels
    group = LANES // part
    size = devices * part
    for tile in range(packed // LANES):
        lanes = slice(tile * LANES, (tile + 1) * LANES)

        @pl.loop(0, devices // group)
        def _(g):
            tiles = [in_ref[g * group + b, :, lanes] for b in range(group)]
            columns = pl.ds(pl.multiple_of(g * LANES, LANES), LANES)
            for a, made in enumerate(swap_blocks(tiles, part)):
                rows = slice((tile * group + a) * modes, (tile * group + a + 1) * modes)
                work[rows, columns] = made

    high_in[...], low_in[...] = split(work[...])
    width = 256

    @pl.loop(0, size // width)
    def _(step):
        columns = pl.ds(pl.multiple_of(step * width, width), width)
        work[:, columns] = dot3(
            (high_in[...], low_in[...]), (high_ref[:, columns], low_ref[:, columns]), ((1,), (0,))
        )

    wide = 512

    @pl.loop(0, size // wide)
    def _(step):
        columns = pl.ds(pl.multiple_of(step * wide, wide), wide)
        for start in range(0, modes, 8):
            shifts = values_x_ref[:, columns] + values_y_ref[start : start + 8, :]
            ratio = partial = None
            for z in range(levels):
                rows = slice(z * modes + start, z * modes + start + 8)
                denom = diag_ref[z] + shifts
                rhs = work[rows, columns]
                if z:
                    denom = denom + coup_ref[z - 1] * ratio
                    rhs = rhs + coup_ref[z - 1] * partial
                inverse = 1.0 / denom
                partial = rhs * inverse
                work[rows, columns] = partial
                if z < levels - 1:
                    ratio = -coup_ref[z] * inverse
                    ratios[rows, columns] = ratio
            solved = partial
            for z in range(levels - 1, -1, -1):
                rows = slice(z * modes + start, z * modes + start + 8)
                if z < levels - 1:
                    solved = work[rows, columns] - ratios[rows, columns] * solved
                work[rows, columns] = solved

    high_in[...], low_in[...] = split(work[...])

    @pl.loop(0, size // width)
    def _(step):
        rows = pl.ds(pl.multiple_of(step * width, width), width)
        work[:, rows] = dot3(
            (high_in[...], low_in[...]), (high_ref[rows, :], low_ref[rows, :]), ((1,), (1,))
        )

    for tile in range(packed // LANES):
        lanes = slice(tile * LANES, (tile + 1) * LANES)

        @pl.loop(0, devices // group)
        def _(g):
            columns = pl.ds(pl.multiple_of(g * LANES, LANES), LANES)
            tiles = [
                work[(tile * group + a) * modes : (tile * group + a + 1) * modes, columns]
                for a in range(group)
            ]
            for b, made in enumerate(swap_blocks(tiles, part)):
                out_ref[g * group + b, :, lanes] = made


def middle(values, high, low, values_x, values_y, diag, coup):
    devices, modes, packed = values.shape
    size = high.shape[0]
    count = modes * diag.shape[0]
    vmem = pl.BlockSpec(memory_space=VMEM)
    smem = pl.BlockSpec(memory_space=pltpu.SMEM)
    return pl.pallas_call(
        middle_kernel,
        out_shape=jax.ShapeDtypeStruct(values.shape, jnp.float32),
        in_specs=[vmem] * 5 + [smem] * 2,
        out_specs=vmem,
        scratch_shapes=[VMEM((count, size), jnp.bfloat16)] * 2
        + [VMEM((count, size), jnp.float32)] * 2,
        compiler_params=pltpu.CompilerParams(vmem_limit_bytes=48 << 20),
    )(values, high, low, values_x[None, :], values_y[:, None], diag, coup)


def shards(
    right_side,
    conduct,
    excavated,
    vectors_x,
    mass_x,
    values_x,
    vectors_y,
    mass_y,
    values_y,
    vertical_diag,
    vertical_coupling,
):
    columns, lines = lax.axis_size("gx"), lax.axis_size("gy")
    devices = columns * lines
    levels, rows, part_y = right_side.shape
    part_x = rows // columns
    modes = vectors_y.shape[1] // devices
    high_x, low_x = split_matrix(vectors_x)
    high_y, low_y = split_matrix(vectors_y)
    start = (lax.axis_index("gy") * columns + lax.axis_index("gx")) * modes
    local_values = lax.dynamic_slice_in_dim(values_y, start, modes, 0)
    adjoint = None
    residual = right_side
    scaled = residual * mass_x[None, :, None] * mass_y[None, None, :]
    scaled = scaled.reshape(levels, columns, part_x, part_y).transpose(1, 0, 2, 3)
    for iteration in range(ITERS):
        scaled = scaled.reshape(columns, levels * part_x, part_y)
        lines_shape = (devices, modes, levels * part_x)
        got = y_transform(
            forward_kernel, ITERS, scaled, high_y, low_y, scaled.shape, lines_shape, True
        )
        solved = middle(
            got, high_x, low_x, values_x, local_values, vertical_diag, vertical_coupling
        )
        back = y_transform(
            inverse_kernel, ITERS + 1, solved, high_y, low_y, scaled.shape, lines_shape, False
        )
        back = back.reshape(columns, levels, part_x, part_y)
        adjoint, residual, *rest = apply_update(
            iteration, back, conduct, excavated, residual, adjoint, mass_x, mass_y
        )
        scaled = rest[0] if rest else None
    return (adjoint, residual)


def solution(mesh):
    in_specs = (
        P(None, "gy", "gx"),
        P(None, "gy", "gx"),
        P(None, "gy", "gx"),
        P(),
        P("gy"),
        P(),
        P(),
        P("gx"),
        P(),
        P(),
        P(),
    )
    out_specs = (P(None, "gy", "gx"), P(None, "gy", "gx"))
    return jax.shard_map(shards, mesh=mesh, in_specs=in_specs, out_specs=out_specs, check_vma=False)
```

```python
import functools
import jax
import jax.numpy as jnp
from jax import lax
from jax.experimental import pallas as pl
from jax.experimental.pallas import tpu as pltpu
from jax.sharding import PartitionSpec as P

ITERS = 2
LANES = 128
VMEM = pltpu.VMEM

storage_term = 0.2


def harmonic(first, second):
    return 2.0 * first * second / (first + second)


def apply_kernel(
    first, scale, back_ref, conduct_ref, active_ref, residual_ref, *refs
):
    refs = list(refs)
    adjoint_ref = None if first else refs.pop(0)
    mass_x_ref, mass_y_ref = (refs.pop(0), refs.pop(0)) if scale else (None, None)
    new_adjoint_ref, new_residual_ref = refs.pop(0), refs.pop(0)
    scaled_ref = refs.pop(0) if scale else None
    masked, held, out_x, in_x, out_y, in_y, send_sem, recv_sem = refs
    levels, rows, part_y = conduct_ref.shape
    columns, part_x = back_ref.shape[0], back_ref.shape[2]
    ix, iy = lax.axis_index("gx"), lax.axis_index("gy")
    nx, ny = lax.axis_size("gx"), lax.axis_size("gy")
    sides = [
        (lax.rem(iy + 1, ny), ix, iy),
        (lax.rem(iy + ny - 1, ny), ix, iy),
        (iy, lax.rem(ix + 1, nx), ix),
        (iy, lax.rem(ix + nx - 1, nx), ix),
    ]
    barrier = pltpu.get_barrier_semaphore()
    for line, column, _ in sides:
        pl.semaphore_signal(
            barrier, inc=1, device_id=(column, line), device_id_type=pl.DeviceIdType.MESH
        )

    out_y[...] = jnp.zeros_like(out_y)
    for plane in (0, levels + 1):
        masked[plane] = jnp.zeros((rows, part_y), jnp.float32)
        held[plane] = jnp.zeros((rows, part_y), jnp.float32)

    @pl.loop(0, levels)
    def _(z):
        update = jnp.concatenate([back_ref[s, z] for s in range(columns)], axis=0)
        value = active_ref[z].astype(jnp.float32) * update
        conduct = conduct_ref[z]
        masked[z + 1] = value
        held[z + 1] = conduct
        for field, plane in enumerate((value, conduct)):
            at = field * levels + z
            out_x[0, pl.ds(at, 1), :] = plane[rows - 1 :, :]
            out_x[1, pl.ds(at, 1), :] = plane[:1, :]
            out_y[0, pl.ds(at, 1), :rows] = jnp.transpose(plane[:, part_y - LANES :])[LANES - 1 :, :]
            out_y[1, pl.ds(at, 1), :rows] = jnp.transpose(plane[:, :LANES])[:1, :]

    pl.semaphore_wait(barrier, 4)
    copies = []
    for k, (line, column, _) in enumerate(sides):
        source, target = (out_x, in_x) if k < 2 else (out_y, in_y)
        copies.append(
            pltpu.make_async_remote_copy(
                src_ref=source.at[k % 2],
                dst_ref=target.at[k % 2],
                send_sem=send_sem.at[k],
                recv_sem=recv_sem.at[k],
                device_id=(column, line),
                device_id_type=pl.DeviceIdType.MESH,
            )
        )
        copies[-1].start()
    for copy in copies:
        copy.wait()

    inside = [
        jnp.where(iy > 0, 1.0, 0.0),
        jnp.where(iy < ny - 1, 1.0, 0.0),
        jnp.where(ix > 0, 1.0, 0.0),
        jnp.where(ix < nx - 1, 1.0, 0.0),
    ]
    row = lax.broadcasted_iota(jnp.int32, (rows, part_y), 0)
    lane = lax.broadcasted_iota(jnp.int32, (rows, part_y), 1)

    def upright(values):
        tall = jnp.transpose(jnp.broadcast_to(values, (LANES, LANES)))[:rows]
        return jnp.concatenate([tall] * (part_y // LANES), axis=1)

    @pl.loop(0, levels)
    def _(z):
        center, conduct = masked[z + 1], held[z + 1]
        result = storage_term * center

        def add(result, other, other_conduct):
            return result + harmonic(conduct, other_conduct) * (center - other)

        result = add(result, masked[z + 2], held[z + 2])
        result = add(result, masked[z], held[z])
        at, at_conduct = pl.ds(z, 1), pl.ds(levels + z, 1)
        result = add(
            result,
            jnp.where(row == rows - 1, in_x[1, at, :], pltpu.roll(center, rows - 1, 0)),
            jnp.where(
                row == rows - 1, in_x[1, at_conduct, :] * inside[1], pltpu.roll(conduct, rows - 1, 0)
            ),
        )
        result = add(
            result,
            jnp.where(row == 0, in_x[0, at, :], pltpu.roll(center, 1, 0)),
            jnp.where(row == 0, in_x[0, at_conduct, :] * inside[0], pltpu.roll(conduct, 1, 0)),
        )
        result = add(
            result,
            jnp.where(lane == part_y - 1, upright(in_y[1, at, :]), pltpu.roll(center, part_y - 1, 1)),
            jnp.where(
                lane == part_y - 1,
                upright(in_y[1, at_conduct, :]) * inside[3],
                pltpu.roll(conduct, part_y - 1, 1),
            ),
        )
        result = add(
            result,
            jnp.where(lane == 0, upright(in_y[0, at, :]), pltpu.roll(center, 1, 1)),
            jnp.where(
                lane == 0, upright(in_y[0, at_conduct, :]) * inside[2], pltpu.roll(conduct, 1, 1)
            ),
        )
        update = jnp.concatenate([back_ref[s, z] for s in range(columns)], axis=0)
        active = active_ref[z].astype(jnp.float32)
        residual = residual_ref[z] - (result + (1.0 - active) * update)
        new_residual_ref[z] = residual
        new_adjoint_ref[z] = update if first else adjoint_ref[z] + update
        if scale:
            scaled = residual * mass_x_ref[...] * mass_y_ref[...]
            for s in range(columns):
                scaled_ref[s, z] = scaled[s * part_x : (s + 1) * part_x, :]


def apply_update(iteration, back, conduct, excavated, residual, adjoint, mass_x, mass_y):
    first, scale = iteration == 0, iteration < ITERS - 1
    levels, rows, part_y = conduct.shape
    operands = [back, conduct, excavated, residual]
    if not first:
        operands.append(adjoint)
    if scale:
        operands += [mass_x[:, None], mass_y[None, :]]
    field = jax.ShapeDtypeStruct(conduct.shape, jnp.float32)
    outputs = [field, field]
    if scale:
        outputs.append(jax.ShapeDtypeStruct(back.shape, jnp.float32))
    vmem = pl.BlockSpec(memory_space=VMEM)
    return pl.pallas_call(
        functools.partial(apply_kernel, first, scale),
        out_shape=outputs,
        in_specs=[vmem] * len(operands),
        out_specs=[vmem] * len(outputs),
        scratch_shapes=[VMEM((levels + 2, rows, part_y), jnp.float32)] * 2
        + [VMEM((2, 2 * levels, part_y), jnp.float32)] * 2
        + [VMEM((2, 2 * levels, LANES), jnp.float32)] * 2
        + [pltpu.SemaphoreType.DMA((4,))] * 2,
        compiler_params=pltpu.CompilerParams(
            collective_id=iteration, has_side_effects=True, vmem_limit_bytes=48 << 20
        ),
    )(*operands)


def split(value):
    high = value.astype(jnp.bfloat16)
    return high, (value - high.astype(jnp.float32)).astype(jnp.bfloat16)


def dot3(first, second, dims):
    def one(a, b):
        return lax.dot_general(a, b, (dims, ((), ())), preferred_element_type=jnp.float32)

    return one(first[0], second[0]) + (one(first[0], second[1]) + one(first[1], second[0]))


def split_matrix(in_ref, high_ref, low_ref):
    height = 64

    @pl.loop(0, in_ref.shape[0] // height)
    def _(step):
        rows = pl.ds(pl.multiple_of(step * height, height), height)
        high_ref[rows, :], low_ref[rows, :] = split(in_ref[rows, :])


MESH = pl.DeviceIdType.MESH


def place():
    columns, lines = lax.axis_size("gx"), lax.axis_size("gy")
    ix, iy = lax.axis_index("gx"), lax.axis_index("gy")
    return columns, columns * lines, ix, iy, iy * columns + ix


def greet_all():
    columns, devices, _, _, me = place()
    barrier = pltpu.get_barrier_semaphore()

    @pl.loop(1, devices)
    def _(k):
        to = lax.rem(me + k, devices)
        pl.semaphore_signal(
            barrier, inc=1, device_id=(lax.rem(to, columns), to // columns), device_id_type=MESH
        )

    pl.semaphore_wait(barrier, devices - 1)


def send_to_all(source_ref, target_ref, lanes, send_sem, recv_sem):
    columns, devices, _, _, me = place()

    @pl.loop(1, devices)
    def _(k):
        to = lax.rem(me + k, devices)
        pltpu.make_async_remote_copy(
            src_ref=source_ref.at[to, :, lanes],
            dst_ref=target_ref.at[me, :, lanes],
            send_sem=send_sem,
            recv_sem=recv_sem,
            device_id=(lax.rem(to, columns), to // columns),
            device_id_type=MESH,
        ).start()


def wait_for_all(ref, lanes, sem):
    part = ref.at[pl.ds(0, ref.shape[0] - 1), :, lanes]
    pltpu.make_async_copy(part, part, sem).wait()


def row_copies(source_ref, target_ref, rows, send_sem, recv_sem):
    columns, _, ix, iy, _ = place()
    copies = []
    for k in range(1, columns):
        to = lax.rem(ix + k, columns)
        copies.append(
            pltpu.make_async_remote_copy(
                src_ref=source_ref.at[to, rows],
                dst_ref=target_ref.at[ix, rows],
                send_sem=send_sem.at[k - 1],
                recv_sem=recv_sem.at[k - 1],
                device_id=(to, iy),
                device_id_type=MESH,
            )
        )
    return copies


def first_forward_kernel(
    in_ref, y_ref, x_ref, out_ref, high_y_ref, low_y_ref, high_x_ref, low_x_ref, *scratch
):
    forward_kernel(
        in_ref, high_y_ref, low_y_ref, out_ref, *scratch,
        before=lambda: split_matrix(y_ref, high_y_ref, low_y_ref),
        after=lambda: split_matrix(x_ref, high_x_ref, low_x_ref),
    )


def forward_kernel(
    in_ref, high_ref, low_ref, out_ref, got, lines, high_in, low_in, send_x, recv_x, send_all, recv_all,
    before=None, after=None,
):
    sources, count, part = in_ref.shape
    devices, modes, _ = out_ref.shape
    _, _, ix, _, me = place()
    chunks = count // LANES
    width = 256
    greet_all()
    copies = []
    for chunk in range(chunks):
        rows = slice(chunk * LANES, (chunk + 1) * LANES)
        copies.append(row_copies(in_ref, got, rows, send_x.at[chunk], recv_x.at[chunk]))
        for copy in copies[-1]:
            copy.start()
    got[ix] = in_ref[ix]
    if before:
        before()
    for chunk in range(chunks):
        rows = slice(chunk * LANES, (chunk + 1) * LANES)
        for copy in copies[chunk]:
            copy.wait_recv()
        for source in range(sources):
            along = slice(source * part, (source + 1) * part)
            high_in[:, along], low_in[:, along] = split(got[source, rows, :])

        @pl.loop(0, devices * modes // width)
        def _(step):
            columns = pl.ds(pl.multiple_of(step * width, width), width)
            made = dot3(
                (high_ref[:, columns], low_ref[:, columns]),
                (high_in[...], low_in[...]),
                ((0,), (1,)),
            )
            blocks = width // modes
            lines[pl.ds(step * blocks, blocks), :, rows] = made.reshape(blocks, modes, LANES)

        send_to_all(lines, out_ref, rows, send_all.at[chunk], recv_all.at[chunk])
        out_ref[me, :, rows] = lines[me, :, rows]
    if after:
        after()
    for chunk in range(chunks):
        rows = slice(chunk * LANES, (chunk + 1) * LANES)
        for copy in copies[chunk]:
            copy.wait_send()
        wait_for_all(lines, rows, send_all.at[chunk])
        wait_for_all(out_ref, rows, recv_all.at[chunk])


def inverse_kernel(
    in_ref, high_ref, low_ref, out_ref, got, made, high_in, low_in, send_x, recv_x, send_all, recv_all
):
    targets, count, part = out_ref.shape
    devices, modes, _ = in_ref.shape
    _, _, ix, _, me = place()
    chunks = count // LANES
    greet_all()
    for chunk in range(chunks):
        rows = slice(chunk * LANES, (chunk + 1) * LANES)
        send_to_all(in_ref, got, rows, send_all.at[chunk], recv_all.at[chunk])
    got[me] = in_ref[me]
    copies = []
    for chunk in range(chunks):
        rows = slice(chunk * LANES, (chunk + 1) * LANES)
        wait_for_all(got, rows, recv_all.at[chunk])
        moved = jnp.transpose(got[:, :, rows].reshape(devices * modes, LANES))
        high_in[...], low_in[...] = split(moved)

        @pl.loop(0, targets)
        def _(target):
            along = pl.ds(pl.multiple_of(target * part, part), part)
            made[target, rows, :] = dot3(
                (high_in[...], low_in[...]), (high_ref[along, :], low_ref[along, :]), ((1,), (1,))
            )

        copies.append(row_copies(made, out_ref, rows, send_x.at[chunk], recv_x.at[chunk]))
        for copy in copies[-1]:
            copy.start()
        out_ref[ix, rows, :] = made[ix, rows, :]
    for chunk in range(chunks):
        rows = slice(chunk * LANES, (chunk + 1) * LANES)
        for copy in copies[chunk]:
            copy.wait()
        wait_for_all(in_ref, rows, send_all.at[chunk])


def y_transform(kernel, collective_id, values, high, low, rows_shape, lines_shape, forward):
    count, size = rows_shape[1], high.shape[0]
    chunks = count // LANES
    rows_vmem, lines_vmem = VMEM(rows_shape, jnp.float32), VMEM(lines_shape, jnp.float32)
    row_sems = pltpu.SemaphoreType.DMA((chunks, rows_shape[0] - 1))
    vmem = pl.BlockSpec(memory_space=VMEM)
    out_shape = jax.ShapeDtypeStruct(lines_shape if forward else rows_shape, jnp.float32)
    out_specs = vmem
    if kernel is first_forward_kernel:
        parts = [jax.ShapeDtypeStruct(matrix.shape, jnp.bfloat16) for matrix in (high, low)]
        out_shape = [out_shape, parts[0], parts[0], parts[1], parts[1]]
        out_specs = [vmem] * 5
    return pl.pallas_call(
        kernel,
        out_shape=out_shape,
        in_specs=[vmem] * 3,
        out_specs=out_specs,
        scratch_shapes=([rows_vmem, lines_vmem] if forward else [lines_vmem, rows_vmem])
        + [VMEM((LANES, size), jnp.bfloat16)] * 2
        + [row_sems] * 2
        + [pltpu.SemaphoreType.DMA((chunks,))] * 2,
        compiler_params=pltpu.CompilerParams(
            collective_id=collective_id, has_side_effects=True, vmem_limit_bytes=48 << 20
        ),
    )(values, high, low)


def swap_blocks(tiles, part):
    count = len(tiles)
    lane = lax.broadcasted_iota(jnp.int32, tiles[0].shape, 1) // part
    result = []
    for a in range(count):
        made = None
        for b in range(count):
            shift = ((b - a) * part) % LANES
            moved = pltpu.roll(tiles[b], shift, 1) if shift else tiles[b]
            made = moved if made is None else jnp.where(lane == b, moved, made)
        result.append(made)
    return result


def middle_kernel(
    in_ref, high_ref, low_ref, values_x_ref, values_y_ref, diag_ref, coup_ref, out_ref,
    high_in, low_in, work, ratios,
):
    devices, modes, packed = in_ref.shape
    levels = diag_ref.shape[0]
    part = packed // levels
    group = LANES // part
    size = devices * part
    for tile in range(packed // LANES):
        lanes = slice(tile * LANES, (tile + 1) * LANES)

        @pl.loop(0, devices // group)
        def _(g):
            tiles = [in_ref[g * group + b, :, lanes] for b in range(group)]
            columns = pl.ds(pl.multiple_of(g * LANES, LANES), LANES)
            for a, made in enumerate(swap_blocks(tiles, part)):
                rows = slice((tile * group + a) * modes, (tile * group + a + 1) * modes)
                work[rows, columns] = made

    high_in[...], low_in[...] = split(work[...])
    width = 256

    @pl.loop(0, size // width)
    def _(step):
        columns = pl.ds(pl.multiple_of(step * width, width), width)
        work[:, columns] = dot3(
            (high_in[...], low_in[...]), (high_ref[:, columns], low_ref[:, columns]), ((1,), (0,))
        )

    wide = 512

    @pl.loop(0, size // wide)
    def _(step):
        columns = pl.ds(pl.multiple_of(step * wide, wide), wide)
        for start in range(0, modes, 8):
            shifts = values_x_ref[:, columns] + values_y_ref[start : start + 8, :]
            ratio = partial = None
            for z in range(levels):
                rows = slice(z * modes + start, z * modes + start + 8)
                denom = diag_ref[z] + shifts
                rhs = work[rows, columns]
                if z:
                    denom = denom + coup_ref[z - 1] * ratio
                    rhs = rhs + coup_ref[z - 1] * partial
                inverse = 1.0 / denom
                partial = rhs * inverse
                work[rows, columns] = partial
                if z < levels - 1:
                    ratio = -coup_ref[z] * inverse
                    ratios[rows, columns] = ratio
            solved = partial
            for z in range(levels - 1, -1, -1):
                rows = slice(z * modes + start, z * modes + start + 8)
                if z < levels - 1:
                    solved = work[rows, columns] - ratios[rows, columns] * solved
                work[rows, columns] = solved

    high_in[...], low_in[...] = split(work[...])

    @pl.loop(0, size // width)
    def _(step):
        rows = pl.ds(pl.multiple_of(step * width, width), width)
        work[:, rows] = dot3(
            (high_in[...], low_in[...]), (high_ref[rows, :], low_ref[rows, :]), ((1,), (1,))
        )

    for tile in range(packed // LANES):
        lanes = slice(tile * LANES, (tile + 1) * LANES)

        @pl.loop(0, devices // group)
        def _(g):
            columns = pl.ds(pl.multiple_of(g * LANES, LANES), LANES)
            tiles = [
                work[(tile * group + a) * modes : (tile * group + a + 1) * modes, columns]
                for a in range(group)
            ]
            for b, made in enumerate(swap_blocks(tiles, part)):
                out_ref[g * group + b, :, lanes] = made


def middle(values, high, low, values_x, values_y, diag, coup):
    devices, modes, packed = values.shape
    size = high.shape[0]
    count = modes * diag.shape[0]
    vmem = pl.BlockSpec(memory_space=VMEM)
    smem = pl.BlockSpec(memory_space=pltpu.SMEM)
    return pl.pallas_call(
        middle_kernel,
        out_shape=jax.ShapeDtypeStruct(values.shape, jnp.float32),
        in_specs=[vmem] * 5 + [smem] * 2,
        out_specs=vmem,
        scratch_shapes=[VMEM((count, size), jnp.bfloat16)] * 2
        + [VMEM((count, size), jnp.float32)] * 2,
        compiler_params=pltpu.CompilerParams(vmem_limit_bytes=48 << 20),
    )(values, high, low, values_x[None, :], values_y[:, None], diag, coup)


def shards(
    right_side,
    conduct,
    excavated,
    vectors_x,
    mass_x,
    values_x,
    vectors_y,
    mass_y,
    values_y,
    vertical_diag,
    vertical_coupling,
):
    columns, lines = lax.axis_size("gx"), lax.axis_size("gy")
    devices = columns * lines
    levels, rows, part_y = right_side.shape
    part_x = rows // columns
    modes = vectors_y.shape[1] // devices
    start = (lax.axis_index("gy") * columns + lax.axis_index("gx")) * modes
    local_values = lax.dynamic_slice_in_dim(values_y, start, modes, 0)
    adjoint = None
    residual = right_side
    scaled = residual * mass_x[None, :, None] * mass_y[None, None, :]
    scaled = scaled.reshape(levels, columns, part_x, part_y).transpose(1, 0, 2, 3)
    for iteration in range(ITERS):
        scaled = scaled.reshape(columns, levels * part_x, part_y)
        lines_shape = (devices, modes, levels * part_x)
        if iteration == 0:
            got, high_y, low_y, high_x, low_x = y_transform(
                first_forward_kernel, ITERS + 2, scaled, vectors_y, vectors_x, scaled.shape,
                lines_shape, True,
            )
        else:
            got = y_transform(
                forward_kernel, ITERS, scaled, high_y, low_y, scaled.shape, lines_shape, True
            )
        solved = middle(
            got, high_x, low_x, values_x, local_values, vertical_diag, vertical_coupling
        )
        back = y_transform(
            inverse_kernel, ITERS + 1, solved, high_y, low_y, scaled.shape, lines_shape, False
        )
        back = back.reshape(columns, levels, part_x, part_y)
        adjoint, residual, *rest = apply_update(
            iteration, back, conduct, excavated, residual, adjoint, mass_x, mass_y
        )
        scaled = rest[0] if rest else None
    return (adjoint, residual)


def solution(mesh):
    in_specs = (
        P(None, "gy", "gx"),
        P(None, "gy", "gx"),
        P(None, "gy", "gx"),
        P(),
        P("gy"),
        P(),
        P(),
        P("gx"),
        P(),
        P(),
        P(),
    )
    out_specs = (P(None, "gy", "gx"), P(None, "gy", "gx"))
    return jax.shard_map(shards, mesh=mesh, in_specs=in_specs, out_specs=out_specs, check_vma=False)
```
